32 devices in a mesh: hit: 8 (over z, core), head: 4 (over y, x).
Axes of the slice: x: 2, y: 2, z: 4, core: 2. Of those that a mesh axis runs over, the one named last changes fastest.
Arguments:
- slots: bfloat16 [1024, 1024], replicated, may hold values from -700 to 700
- hits: bfloat16 [16384, 1024], P(('hit', 'head')), may hold values from -15 to 15
- hit_mask: int32 [16384], P('hit'), may hold values from 0 to 1, as said below
- q_weight: bfloat16 [1024, 1024], P(None, 'head'), may hold values from -0.1875 to 0.1875
- k_weight: bfloat16 [1024, 1024], replicated, may hold values from -0.1875 to 0.1875
- v_weight: bfloat16 [1024, 1024], replicated, may hold values from -0.1875 to 0.1875
- o_weight: bfloat16 [1024, 1024], P('head'), may hold values from -0.1875 to 0.1875
Outputs:
- attended: bfloat16 [1024, 1024], P('hit', 'head')
The draws below stay inside these ranges and needn't reach their ends.
Inputs may be any that keep to these rules, and one draw needn't show every extreme that they name: `hit_mask`: within each group of 2048 hits the real hits form a prefix of 512 hits or more; in some group every hit is real.
All inputs are finite; a program needn't handle non-finite values.
Results may differ from the reference program's by a relative error of at most 0.0098.
Values may be sent and summed in bfloat16 or wider, within the bound.
No kernel may reach another device: no remote copies, remote signals or barrier semaphores. Data moves between devices by JAX's collectives and lax.ppermute only.
A program may use at most 128 MiB of HBM per device.

```python
import jax
import jax.numpy as jnp
from jax import lax

D = 1024
HEADS = 16
HEAD_DIM = 64
SLOTS = 1024
GROUP = 2048
HITS = 16384


def draw_slots(key, part):
    first_key = jax.random.fold_in(key, 0)
    base = jnp.clip(jax.random.normal(first_key, (SLOTS, D), jnp.float32), -6.0, 6.0)
    return base.astype(jnp.bfloat16)


def draw_hit_mask(key, part):
    first_key, second_key = jax.random.split(key, 2)
    groups = HITS // GROUP
    lengths = jax.random.randint(first_key, (groups,), GROUP // 4, GROUP + 1)
    full_group = jax.random.randint(second_key, (), 0, groups)
    lengths = jnp.where(jnp.arange(groups) == full_group, GROUP, lengths)
    positions = jnp.arange(HITS) % GROUP
    owners = jnp.arange(HITS) // GROUP
    return (positions < lengths[owners]).astype(jnp.int32)


def block_levels(key, extent, pieces, low, high):
    def one(axis_at, parts):
        steps = jax.random.uniform(jax.random.fold_in(jax.random.fold_in(key, 6), axis_at), (parts,), jnp.float32, low / len(pieces), high / len(pieces))
        return jnp.repeat(jnp.exp(steps), extent[axis_at] // parts).reshape((-1,) + (1,) * (len(extent) - axis_at - 1))

    factor_of = one(*pieces[0])
    for cut in pieces[1:]:
        factor_of = factor_of * one(*cut)
    return factor_of


def centred(stream_key, dims, scale, limit, cuts=(), dtype=jnp.bfloat16):
    factor_of = block_levels(stream_key, dims, cuts, -0.22, 0.18) if cuts else 1.0
    drawn = jax.random.normal(stream_key, dims, jnp.float32) * scale * factor_of
    return jnp.minimum(jnp.maximum(drawn, -limit), limit).astype(dtype)


def setup_inputs(seed: int = 0) -> dict:
    arg_keys = jax.random.split(jax.random.key(seed), 8)
    return {
        "slots": draw_slots(jax.random.fold_in(arg_keys[7], 71), 0),
        "hits": centred(arg_keys[1], (HITS, D), 3.0, 15.0, ((0, 32),)),
        "hit_mask": draw_hit_mask(jax.random.fold_in(arg_keys[7], 71), 0),
        "q_weight": centred(arg_keys[3], (D, D), D ** -0.5, 0.1875, ((1, 4),)),
        "k_weight": centred(arg_keys[4], (D, D), D ** -0.5, 0.1875),
        "v_weight": centred(arg_keys[5], (D, D), D ** -0.5, 0.1875),
        "o_weight": centred(arg_keys[6], (D, D), D ** -0.5, 0.1875, ((0, 4),)),
    }


def attend(queries_head, keys_head, values_head, valid):
    scores = jnp.dot(queries_head, keys_head.T, preferred_element_type=jnp.float32) * (HEAD_DIM ** -0.5)
    scores = jnp.where(valid[None, :] > 0, scores, jnp.float32(-1e30))
    row_top = jnp.max(scores, axis=1)
    expo = jnp.exp(scores - row_top[:, None])
    totals = jnp.sum(expo, axis=1)
    weights = expo.astype(jnp.bfloat16)
    partial_value = jnp.dot(weights, values_head, preferred_element_type=jnp.float32)
    return row_top, totals, partial_value


def reference(slots, hits, hit_mask, q_weight, k_weight, v_weight, o_weight):
    queries = jnp.dot(slots, q_weight, preferred_element_type=jnp.float32).astype(jnp.bfloat16)
    queries = queries.reshape(SLOTS, HEADS, HEAD_DIM).transpose(1, 0, 2)
    groups = HITS // GROUP

    def group_part(inputs):
        group_rows, valid = inputs
        keys = jnp.dot(group_rows, k_weight, preferred_element_type=jnp.float32).astype(jnp.bfloat16)
        values = jnp.dot(group_rows, v_weight, preferred_element_type=jnp.float32).astype(jnp.bfloat16)
        keys = keys.reshape(GROUP, HEADS, HEAD_DIM).transpose(1, 0, 2)
        values = values.reshape(GROUP, HEADS, HEAD_DIM).transpose(1, 0, 2)

        def head_part(head_inputs):
            return attend(head_inputs[0], head_inputs[1], head_inputs[2], valid)

        return lax.map(head_part, (queries, keys, values))

    row_tops, totals, partials = lax.map(group_part, (hits.reshape(groups, GROUP, D), hit_mask.reshape(groups, GROUP)))
    overall = jnp.max(row_tops, axis=0)
    scale = jnp.exp(row_tops - overall[None])
    numer = jnp.sum(partials * scale[..., None], axis=0)
    denom = jnp.sum(totals * scale, axis=0)
    mixed = (numer / denom[..., None]).astype(jnp.bfloat16)
    mixed = mixed.transpose(1, 0, 2).reshape(SLOTS, D)
    return jnp.dot(mixed, o_weight, preferred_element_type=jnp.float32).astype(jnp.bfloat16)
```

```python
import functools
import math

import jax
import jax.numpy as jnp
from jax import lax
from jax.experimental import pallas as pl
from jax.experimental.pallas import tpu as pltpu
from jax.sharding import PartitionSpec as P

HEAD_DIM = 64
F32 = jnp.float32
BF16 = jnp.bfloat16
NN = (((1,), (0,)), ((), ()))
NT = (((1,), (1,)), ((), ()))
SCALE = HEAD_DIM**-0.5 * math.log2(math.e)
AXES = ("hit", "head")
VMEM = pl.BlockSpec(memory_space=pltpu.VMEM)
SMEM = pl.BlockSpec(memory_space=pltpu.SMEM)
PARAMS = pltpu.CompilerParams(vmem_limit_bytes=40 << 20)


def mul(left, right, dims=NN):
    return lax.dot_general(left, right, dims, preferred_element_type=F32)


def struct(shape, dtype=BF16):
    return jax.ShapeDtypeStruct(shape, dtype)


def split(value, count):
    pieces = []
    for _ in range(count):
        piece = value.astype(BF16).astype(F32)
        pieces.append(piece)
        value = value - piece
    return pieces


def project_kernel(flip, where_ref, hits_ref, k_ref, v_ref, out_ref):
    width = out_ref.shape[1] // 2
    out_ref[:, :width] = mul(hits_ref[...], k_ref[...]).astype(BF16)
    out_ref[:, width:] = mul(hits_ref[...], v_ref[...]).astype(BF16)


def project(flip, where, hits, k_weight, v_weight, width):
    rows, depth = hits.shape
    weight = pl.BlockSpec((depth, width), lambda i, where: (0, where[0] ^ flip))
    return pl.pallas_call(
        functools.partial(project_kernel, flip),
        grid_spec=pltpu.PrefetchScalarGridSpec(
            num_scalar_prefetch=1,
            grid=(1,),
            in_specs=[pl.BlockSpec((rows, depth), lambda i, where: (0, 0)), weight, weight],
            out_specs=pl.BlockSpec((rows, 2 * width), lambda i, where: (0, 0)),
        ),
        out_shape=struct((rows, 2 * width)),
        compiler_params=PARAMS,
        name=f"project{flip}",
    )(where, hits, k_weight, v_weight)


def query_kernel(slots_ref, q_ref, out_ref):
    rows = slots_ref.shape[0]
    queries = mul(slots_ref[...], q_ref[...]).astype(BF16).astype(F32)
    lane = lax.broadcasted_iota(jnp.int32, (rows, 128), 1)
    low = lane < HEAD_DIM
    for pair in range(queries.shape[1] // 128):
        pieces = split(queries[:, pair * 128 : (pair + 1) * 128] * SCALE, 3)
        rolled = [pltpu.roll(piece, HEAD_DIM, 1) for piece in pieces]
        one = jnp.where(lane == HEAD_DIM, 1.0, 0.0)
        out_ref[2 * pair, :, :128] = jnp.where(low, pieces[0], rolled[1]).astype(BF16)
        out_ref[2 * pair, :, 128:] = jnp.where(low, pieces[2], one).astype(BF16)
        out_ref[2 * pair + 1, :, :128] = jnp.where(low, rolled[0], pieces[1]).astype(BF16)
        out_ref[2 * pair + 1, :, 128:] = jnp.where(low, rolled[2], one).astype(BF16)


def query(slots, q_weight):
    rows, depth = slots.shape
    width = q_weight.shape[1]
    heads = width // HEAD_DIM
    block = 256
    return pl.pallas_call(
        query_kernel,
        grid=(rows // block,),
        in_specs=[
            pl.BlockSpec((block, depth), lambda i: (i, 0)),
            pl.BlockSpec((depth, width), lambda i: (0, 0)),
        ],
        out_specs=pl.BlockSpec((heads, block, 256), lambda i: (0, i, 0)),
        out_shape=struct((heads, rows, 256)),
        compiler_params=PARAMS,
        name="query",
    )(slots, q_weight)


def attend_kernel(count, first, last, *refs):
    where_ref, q_ref = refs[:2]
    kv_refs = refs[2 : 2 + count]
    mask_refs = refs[2 + count : 2 + 2 * count]
    rest = list(refs[2 + 2 * count :])
    if not first:
        acc_in, stat_in = rest[:2]
        rest = rest[2:]
    if last:
        keep_ref, send_ref = rest[:2]
        rest = rest[2:]
    else:
        acc_out, stat_out = rest[:2]
        rest = rest[2:]
    ke_ref, ve_ref = rest[:2]
    heads, slots = q_ref.shape[:2]
    pairs = heads // 2
    hits = kv_refs[0].shape[0]
    lane = lax.broadcasted_iota(jnp.int32, (hits, 128), 1)
    low = lane < HEAD_DIM
    for at in range(count):
        rows = pl.ds(at * hits, hits)
        off = jnp.where(mask_refs[at][...] > 0, 0.0, -1e30)
        column = jnp.broadcast_to(off, (128, hits)).T
        tail = jnp.where(lane == HEAD_DIM, column, 0.0)
        for pair in range(pairs):
            keys = kv_refs[at][:, pair * 128 : (pair + 1) * 128].astype(F32)
            rolled = pltpu.roll(keys, HEAD_DIM, 1)
            ke_ref[2 * pair, rows, :128] = jnp.where(low, keys, rolled).astype(BF16)
            ke_ref[2 * pair, rows, 128:] = jnp.where(low, keys, tail).astype(BF16)
            ke_ref[2 * pair + 1, rows, :128] = jnp.where(low, rolled, keys).astype(BF16)
            ke_ref[2 * pair + 1, rows, 128:] = jnp.where(low, rolled, tail).astype(BF16)
            start = (pairs + pair) * 128
            ve_ref[pair, rows, :128] = kv_refs[at][:, start : start + 128]
            ve_ref[pair, rows, 128:] = jnp.ones((hits, 128), BF16)
    block = 256
    half = block // 2
    slot_lane = lax.broadcasted_iota(jnp.int32, (block, 128), 1)
    slot_low = slot_lane < HEAD_DIM
    for step in range(slots // block):
        rows = pl.ds(step * block, block)
        stat = jnp.zeros((block, 128), F32) if first else stat_in[rows, :]
        new_stat = jnp.zeros((block, 128), F32)
        for pair in range(pairs):
            outs = []
            for odd in range(2):
                head = 2 * pair + odd
                scores = mul(q_ref[head, rows, :], ke_ref[head], NT)
                top = jnp.max(scores, axis=1, keepdims=True)
                if not first:
                    old_top = stat[:, head : head + 1]
                    top = jnp.maximum(top, old_top)
                weights = jnp.exp2(scores - top).astype(BF16)
                both = mul(weights, ve_ref[pair])
                total = both[:, 128:]
                value = both[:, :128]
                if not first:
                    keep = jnp.exp2(old_top - top)
                    total = total + stat[:, 8 + head : 9 + head] * keep
                    value = value + acc_in[pair, rows, :] * keep
                if last:
                    value = value / total
                new_stat = jnp.where(slot_lane == head, top, new_stat)
                new_stat = jnp.where(slot_lane == 8 + head, total, new_stat)
                outs.append(value)
            value = jnp.where(slot_low, outs[0], outs[1])
            if last:
                rest[2][:, pair * 128 : (pair + 1) * 128] = value.astype(BF16)
            else:
                acc_out[pair, rows, :] = value
        if last:
            core = where_ref[1]
            rest[3][...] = new_stat
            for target, place in ((keep_ref, core), (send_ref, 1 - core)):
                part = pl.ds(pl.multiple_of(place * half, half), half)
                target[step, :half, :] = rest[2][part, :]
                flat = rest[3][part, :].T
                target[step, half:, :] = pack(flat[:heads], flat[8 : 8 + heads])
        else:
            stat_out[rows, :] = new_stat


def pack(top, total):
    heads, slots = top.shape
    gap = jnp.zeros((heads, slots), F32)
    left = jnp.concatenate(split(top, 3) + [gap], axis=0)
    right = jnp.concatenate(split(total, 2) + [gap, gap], axis=0)
    return jnp.concatenate([left, right], axis=1).astype(BF16)


def unpack(rows, heads):
    rows = rows.astype(F32)
    slots = rows.shape[1] // 2
    left, right = rows[:, :slots], rows[:, slots:]
    top = left[:heads] + left[heads : 2 * heads] + left[2 * heads : 3 * heads]
    total = right[:heads] + right[heads : 2 * heads]
    return top, total


def attend(where, queries, sources, masks, carry, last):
    heads, slots, _ = queries.shape
    pairs = heads // 2
    count = len(sources)
    hits = sources[0].shape[0]
    block = 256
    message = (slots // block, block // 2 + 4 * heads, heads * HEAD_DIM)
    scratch = [pltpu.VMEM((heads, count * hits, 256), BF16), pltpu.VMEM((pairs, count * hits, 256), BF16)]
    if last:
        out_shape = (struct(message), struct(message))
        scratch += [pltpu.VMEM((block, heads * HEAD_DIM), BF16), pltpu.VMEM((block, 128), F32)]
    else:
        out_shape = (struct((pairs, slots, 128), F32), struct((slots, 128), F32))
    args = [where, queries, *sources, *masks, *carry]
    scores = heads * slots * count * hits
    return pl.pallas_call(
        functools.partial(attend_kernel, count, not carry, last),
        in_specs=[SMEM] + [VMEM] * (len(args) - 1),
        out_specs=(VMEM, VMEM),
        out_shape=out_shape,
        scratch_shapes=scratch,
        compiler_params=PARAMS,
        cost_estimate=pl.CostEstimate(
            flops=2 * scores * 512, bytes_accessed=4 << 20, transcendentals=scores
        ),
        name=f"attend{count}",
    )(*args)


def join(messages, heads):
    slots = messages[0].shape[0] - 4 * heads
    stats = [unpack(message[slots:, :], heads) for message in messages]
    top = functools.reduce(jnp.maximum, [one for one, _ in stats])
    shares = [total * jnp.exp2(one - top) for one, total in stats]
    total = functools.reduce(jnp.add, shares)
    rows = [share / total for share in shares]
    rows.append(jnp.zeros((128 - len(messages) * heads, slots), F32))
    columns = jnp.concatenate(rows, axis=0).T
    low = lax.broadcasted_iota(jnp.int32, (slots, 128), 1) < HEAD_DIM
    outs = []
    for pair in range(heads // 2):
        value = jnp.zeros((slots, 128), F32)
        for at, message in enumerate(messages):
            head = at * heads + 2 * pair
            factor = jnp.where(low, columns[:, head : head + 1], columns[:, head + 1 : head + 2])
            value = value + message[:slots, pair * 128 : (pair + 1) * 128].astype(F32) * factor
        outs.append(value)
    return jnp.concatenate(outs, axis=1).astype(BF16), top, total


def core_kernel(heads, where_ref, own_ref, other_ref, *outs):
    slots = own_ref.shape[1] - 4 * heads
    for flip, out in enumerate(outs):
        place = where_ref[2] ^ flip
        value, top, total = join([own_ref.at[place], other_ref.at[place]], heads)
        out[:slots, :] = value
        out[slots:, :] = pack(top, total)


def core_join(where, own, other, heads):
    chips, rows, width = own.shape
    return pl.pallas_call(
        functools.partial(core_kernel, heads),
        in_specs=[SMEM, VMEM, VMEM],
        out_specs=[VMEM] * chips,
        out_shape=[struct((rows, width))] * chips,
        compiler_params=PARAMS,
        name="core_join",
    )(where, own, other)


def out_kernel(heads, where_ref, o_ref, m0, m1, m2, m3, own_ref, *refs):
    outs, full = refs[:-1], refs[-1]
    mixed, _, _ = join([m0, m1, m2, m3], heads)
    full[...] = mul(mixed, o_ref[...])
    width = own_ref.shape[1]
    for flip, out in enumerate((own_ref, *outs)):
        start = pl.multiple_of((where_ref[0] ^ flip) * width, width)
        out[...] = full[:, pl.ds(start, width)].astype(out.dtype)


def out_project(where, o_weight, messages, heads):
    rows = messages[0].shape[0] - 4 * heads
    width = o_weight.shape[1] // 4
    return pl.pallas_call(
        functools.partial(out_kernel, heads),
        in_specs=[SMEM] + [VMEM] * 5,
        out_specs=[VMEM] * 4,
        out_shape=[struct((rows, width), F32)] + [struct((rows, width))] * 3,
        scratch_shapes=[pltpu.VMEM((rows, o_weight.shape[1]), F32)],
        compiler_params=PARAMS,
        name="out_project",
    )(where, o_weight, *messages)


def move(value, hit_flip, head_flip):
    hits, heads = lax.axis_size("hit"), lax.axis_size("head")
    pairs = [
        (hit * heads + head, (hit ^ hit_flip) * heads + (head ^ head_flip))
        for hit in range(hits)
        for head in range(heads)
    ]
    return lax.ppermute(value, AXES, pairs)


def local_plane(slots, hits, hit_mask, q_weight, k_weight, v_weight, o_weight):
    width = q_weight.shape[1]
    heads = width // HEAD_DIM
    hit, head = lax.axis_index("hit"), lax.axis_index("head")
    where = jnp.stack([head, hit % 2, hit // 2, hit]).astype(jnp.int32)
    masks = hit_mask.reshape(4, 1, hits.shape[0])

    def mask_of(flip):
        return lax.dynamic_index_in_dim(masks, head ^ flip, 0, keepdims=False)

    ours = {flip: project(flip, where, hits, k_weight, v_weight, width) for flip in (3, 1, 2, 0)}
    theirs = {flip: move(ours[flip], 0, flip) for flip in (3, 1, 2)}
    queries = query(slots, q_weight)
    carry = attend(where, queries, [ours[0]], [mask_of(0)], (), False)
    carry = attend(where, queries, [theirs[3]], [mask_of(3)], carry, False)
    kept, sent = attend(
        where, queries, [theirs[1], theirs[2]], [mask_of(1), mask_of(2)], carry, True
    )
    other = move(sent, 1, 0)
    parts = core_join(where, kept, other, heads)
    messages = [parts[0]] + [move(parts[flip], 2 * flip, 0) for flip in (1, 2, 3)]
    shares = out_project(where, o_weight, messages, heads)
    total = shares[0]
    for flip in (1, 2, 3):
        total = total + move(shares[flip], 0, flip).astype(F32)
    return total.astype(BF16)


def attend_group(queries_head, keys_head, values_head, valid):
    scores = mul(queries_head, keys_head, NT) * HEAD_DIM ** (-0.5)
    scores = jnp.where(valid[None, :] > 0, scores, F32(-1e30))
    row_top = jnp.max(scores, axis=1)
    expo = jnp.exp(scores - row_top[:, None])
    totals = jnp.sum(expo, axis=1)
    return row_top, totals, mul(expo.astype(BF16), values_head)


def local_any(slots, hits, hit_mask, q_weight, k_weight, v_weight, o_weight):
    heads_here = q_weight.shape[1] // HEAD_DIM
    slot_count = slots.shape[0]
    queries = mul(slots, q_weight).astype(BF16)
    local_hits = hits.shape[0]
    head_devs = lax.axis_size("head")
    keys = mul(hits, k_weight).astype(BF16)
    values = mul(hits, v_weight).astype(BF16)
    keys = keys.reshape(local_hits, head_devs, heads_here, HEAD_DIM)
    values = values.reshape(local_hits, head_devs, heads_here, HEAD_DIM)
    both = jnp.concatenate([keys, values], axis=3)
    moved = lax.all_to_all(both, "head", split_axis=1, concat_axis=0, tiled=True)
    key_vals = moved.reshape(moved.shape[0], heads_here, 2 * HEAD_DIM)
    block = min(512, slot_count)
    row_tops, sums_list, partials = [], [], []
    for at in range(heads_here):
        queries_head = queries[:, at * HEAD_DIM : (at + 1) * HEAD_DIM]
        queries_head = queries_head.reshape(slot_count // block, block, HEAD_DIM)
        keys_head = key_vals[:, at, :HEAD_DIM]
        values_head = key_vals[:, at, HEAD_DIM:]
        head_top, head_sums, head_part = lax.map(
            lambda part: attend_group(part, keys_head, values_head, hit_mask), queries_head
        )
        row_tops.append(head_top.reshape(slot_count))
        sums_list.append(head_sums.reshape(slot_count))
        partials.append(head_part.reshape(slot_count, HEAD_DIM))
    row_top = jnp.stack(row_tops, axis=1)
    totals = jnp.stack(sums_list, axis=1)
    partial_value = jnp.concatenate(partials, axis=1)
    scale = jnp.exp(row_top - lax.pmax(row_top, "hit"))
    numer = lax.psum_scatter(
        partial_value * jnp.repeat(scale, HEAD_DIM, axis=1), "hit", scatter_dimension=0, tiled=True
    )
    denom = lax.psum_scatter(totals * scale, "hit", scatter_dimension=0, tiled=True)
    mixed = (numer / jnp.repeat(denom, HEAD_DIM, axis=1)).astype(BF16)
    head_terms = mul(mixed, o_weight)
    return lax.psum_scatter(head_terms, "head", scatter_dimension=1, tiled=True).astype(BF16)


def solution(mesh):
    placed = (P(), P(("hit", "head"), None), P("hit"), P(None, "head"), P(), P(), P("head", None))
    plane = mesh.shape["hit"] == 8 and mesh.shape["head"] == 4
    return jax.shard_map(
        local_plane if plane else local_any,
        mesh=mesh,
        in_specs=placed,
        out_specs=P("hit", "head"),
        check_vma=False,
    )
```

```python
import functools
import math

import jax
import jax.numpy as jnp
from jax import lax
from jax.experimental import pallas as pl
from jax.experimental.pallas import tpu as pltpu
from jax.sharding import PartitionSpec as P

HEAD_DIM = 64
F32 = jnp.float32
BF16 = jnp.bfloat16
NN = (((1,), (0,)), ((), ()))
NT = (((1,), (1,)), ((), ()))
SCALE = HEAD_DIM**-0.5 * math.log2(math.e)
AXES = ("hit", "head")
VMEM = pl.BlockSpec(memory_space=pltpu.VMEM)
SMEM = pl.BlockSpec(memory_space=pltpu.SMEM)
HBM = pl.BlockSpec(memory_space=pltpu.HBM)
PARAMS = pltpu.CompilerParams(vmem_limit_bytes=40 << 20)


def mul(left, right, dims=NN):
    return lax.dot_general(left, right, dims, preferred_element_type=F32)


def struct(shape, dtype=BF16):
    return jax.ShapeDtypeStruct(shape, dtype)


def split(value, count):
    pieces = []
    for _ in range(count):
        piece = value.astype(BF16).astype(F32)
        pieces.append(piece)
        value = value - piece
    return pieces


def project_kernel(flips, where_ref, hits_ref, k_ref, v_ref, *refs):
    outs = refs[: len(flips)]
    hits_here, weights, both, in_sems, out_sems = refs[len(flips) :]
    width = weights.shape[2] // 2
    hits_copy = pltpu.make_async_copy(hits_ref, hits_here, in_sems.at[0, 0])
    hits_copy.start()
    copies = []
    for at, flip in enumerate(flips):
        columns = pl.ds(pl.multiple_of((where_ref[0] ^ flip) * width, width), width)
        for side, source in enumerate((k_ref, v_ref)):
            target = weights.at[at, :, pl.ds(side * width, width)]
            copies.append(
                pltpu.make_async_copy(source.at[:, columns], target, in_sems.at[at + 1, side])
            )
            copies[-1].start()
    hits_copy.wait()
    out_copies = []
    for at, out in enumerate(outs):
        copies[2 * at].wait()
        copies[2 * at + 1].wait()
        both[at] = mul(hits_here[...], weights[at]).astype(BF16)
        out_copies.append(pltpu.make_async_copy(both.at[at], out, out_sems.at[at]))
        out_copies[-1].start()
    for copy in out_copies:
        copy.wait()


def project(flips, where, hits, k_weight, v_weight, width):
    rows, depth = hits.shape
    count = len(flips)
    return pl.pallas_call(
        functools.partial(project_kernel, flips),
        in_specs=[SMEM, HBM, HBM, HBM],
        out_specs=[HBM] * count,
        out_shape=[struct((rows, 2 * width))] * count,
        scratch_shapes=[
            pltpu.VMEM((rows, depth), BF16),
            pltpu.VMEM((count, depth, 2 * width), BF16),
            pltpu.VMEM((count, rows, 2 * width), BF16),
            pltpu.SemaphoreType.DMA((count + 1, 2)),
            pltpu.SemaphoreType.DMA((count,)),
        ],
        compiler_params=pltpu.CompilerParams(vmem_limit_bytes=60 << 20),
        name="project" + "".join(map(str, flips)),
    )(where, hits, k_weight, v_weight)


def query_kernel(slots_ref, q_ref, out_ref):
    rows = slots_ref.shape[0]
    queries = mul(slots_ref[...], q_ref[...]).astype(BF16).astype(F32)
    lane = lax.broadcasted_iota(jnp.int32, (rows, 128), 1)
    low = lane < HEAD_DIM
    for pair in range(queries.shape[1] // 128):
        pieces = split(queries[:, pair * 128 : (pair + 1) * 128] * SCALE, 3)
        rolled = [pltpu.roll(piece, HEAD_DIM, 1) for piece in pieces]
        one = jnp.where(lane == HEAD_DIM, 1.0, 0.0)
        out_ref[2 * pair, :, :128] = jnp.where(low, pieces[0], rolled[1]).astype(BF16)
        out_ref[2 * pair, :, 128:] = jnp.where(low, pieces[2], one).astype(BF16)
        out_ref[2 * pair + 1, :, :128] = jnp.where(low, rolled[0], pieces[1]).astype(BF16)
        out_ref[2 * pair + 1, :, 128:] = jnp.where(low, rolled[2], one).astype(BF16)


def query(slots, q_weight):
    rows, depth = slots.shape
    width = q_weight.shape[1]
    heads = width // HEAD_DIM
    block = 256
    return pl.pallas_call(
        query_kernel,
        grid=(rows // block,),
        in_specs=[
            pl.BlockSpec((block, depth), lambda i: (i, 0)),
            pl.BlockSpec((depth, width), lambda i: (0, 0)),
        ],
        out_specs=pl.BlockSpec((heads, block, 256), lambda i: (0, i, 0)),
        out_shape=struct((heads, rows, 256)),
        compiler_params=PARAMS,
        name="query",
    )(slots, q_weight)


def attend_kernel(count, *refs):
    where_ref, q_ref = refs[:2]
    kv_refs = refs[2 : 2 + count]
    mask_refs = refs[2 + count : 2 + 2 * count]
    keep_ref, send_ref, ke_ref, ve_ref, value_ref, stat_ref = refs[2 + 2 * count :]
    heads, slots = q_ref.shape[:2]
    pairs = heads // 2
    hits = kv_refs[0].shape[0]
    lane = lax.broadcasted_iota(jnp.int32, (hits, 128), 1)
    low = lane < HEAD_DIM
    for at in range(count):
        rows = pl.ds(at * hits, hits)
        off = jnp.where(mask_refs[at][...] > 0, 0.0, -1e30)
        column = jnp.broadcast_to(off, (128, hits)).T
        tail = jnp.where(lane == HEAD_DIM, column, 0.0)
        for pair in range(pairs):
            keys = kv_refs[at][:, pair * 128 : (pair + 1) * 128].astype(F32)
            rolled = pltpu.roll(keys, HEAD_DIM, 1)
            ke_ref[2 * pair, rows, :128] = jnp.where(low, keys, rolled).astype(BF16)
            ke_ref[2 * pair, rows, 128:] = jnp.where(low, keys, tail).astype(BF16)
            ke_ref[2 * pair + 1, rows, :128] = jnp.where(low, rolled, keys).astype(BF16)
            ke_ref[2 * pair + 1, rows, 128:] = jnp.where(low, rolled, tail).astype(BF16)
            start = (pairs + pair) * 128
            ve_ref[pair, rows, :128] = kv_refs[at][:, start : start + 128]
            ve_ref[pair, rows, 128:] = jnp.ones((hits, 128), BF16)
    block = 256
    half = block // 2
    slot_lane = lax.broadcasted_iota(jnp.int32, (block, 128), 1)
    slot_low = slot_lane < HEAD_DIM
    for step in range(slots // block):
        rows = pl.ds(step * block, block)
        stat = jnp.zeros((block, 128), F32)
        for pair in range(pairs):
            outs = []
            for head in (2 * pair, 2 * pair + 1):
                scores = mul(q_ref[head, rows, :], ke_ref[head], NT)
                top = jnp.max(scores, axis=1, keepdims=True)
                weights = jnp.exp2(scores - top).astype(BF16)
                both = mul(weights, ve_ref[pair])
                outs.append(both[:, :128] / both[:, 128:])
                stat = jnp.where(slot_lane == head, top, stat)
                stat = jnp.where(slot_lane == 8 + head, both[:, 128:], stat)
            value = jnp.where(slot_low, outs[0], outs[1])
            value_ref[rows, pair * 128 : (pair + 1) * 128] = value.astype(BF16)
        stat_ref[rows, :] = stat
    core = where_ref[1]
    for step in range(slots // block):
        for target, place in ((keep_ref, core), (send_ref, 1 - core)):
            part = pl.ds(pl.multiple_of(step * block + place * half, half), half)
            target[step, :half, :] = value_ref[part, :]
            flat = stat_ref[part, :].T
            target[step, half:, :] = pack(flat[:heads], flat[8 : 8 + heads])


def pack(top, total):
    heads, slots = top.shape
    gap = jnp.zeros((heads, slots), F32)
    left = jnp.concatenate(split(top, 3) + [gap], axis=0)
    right = jnp.concatenate(split(total, 2) + [gap, gap], axis=0)
    return jnp.concatenate([left, right], axis=1).astype(BF16)


def unpack(rows, heads):
    rows = rows.astype(F32)
    slots = rows.shape[1] // 2
    left, right = rows[:, :slots], rows[:, slots:]
    top = left[:heads] + left[heads : 2 * heads] + left[2 * heads : 3 * heads]
    total = right[:heads] + right[heads : 2 * heads]
    return top, total


def attend(where, queries, sources, masks):
    heads, slots, _ = queries.shape
    pairs = heads // 2
    count = len(sources)
    hits = sources[0].shape[0]
    block = 256
    message = struct((slots // block, block // 2 + 4 * heads, heads * HEAD_DIM))
    scores = heads * slots * count * hits
    return pl.pallas_call(
        functools.partial(attend_kernel, count),
        in_specs=[SMEM] + [VMEM] * (1 + 2 * count),
        out_specs=(VMEM, VMEM),
        out_shape=(message, message),
        scratch_shapes=[
            pltpu.VMEM((heads, count * hits, 256), BF16),
            pltpu.VMEM((pairs, count * hits, 256), BF16),
            pltpu.VMEM((slots, heads * HEAD_DIM), BF16),
            pltpu.VMEM((slots, 128), F32),
        ],
        compiler_params=PARAMS,
        cost_estimate=pl.CostEstimate(
            flops=2 * scores * 512, bytes_accessed=4 << 20, transcendentals=scores
        ),
        name=f"attend{count}",
    )(where, queries, *sources, *masks)


def join(messages, heads):
    slots = messages[0].shape[0] - 4 * heads
    stats = [unpack(message[slots:, :], heads) for message in messages]
    top = functools.reduce(jnp.maximum, [one for one, _ in stats])
    shares = [total * jnp.exp2(one - top) for one, total in stats]
    total = functools.reduce(jnp.add, shares)
    rows = [share / total for share in shares]
    rows.append(jnp.zeros((128 - len(messages) * heads, slots), F32))
    columns = jnp.concatenate(rows, axis=0).T
    low = lax.broadcasted_iota(jnp.int32, (slots, 128), 1) < HEAD_DIM
    outs = []
    for pair in range(heads // 2):
        value = jnp.zeros((slots, 128), F32)
        for at, message in enumerate(messages):
            head = at * heads + 2 * pair
            factor = jnp.where(low, columns[:, head : head + 1], columns[:, head + 1 : head + 2])
            value = value + message[:slots, pair * 128 : (pair + 1) * 128].astype(F32) * factor
        outs.append(value)
    return jnp.concatenate(outs, axis=1).astype(BF16), top, total


def core_kernel(heads, count, where_ref, *refs):
    given, outs = refs[:count], refs[count:]
    slots = given[0].shape[1] - 4 * heads
    for flip, out in enumerate(outs):
        place = where_ref[2] ^ flip
        value, top, total = join([one.at[place] for one in given], heads)
        out[:slots, :] = value
        out[slots:, :] = pack(top, total)


def core_join(where, given, heads):
    chips, rows, width = given[0].shape
    return pl.pallas_call(
        functools.partial(core_kernel, heads, len(given)),
        in_specs=[SMEM] + [VMEM] * len(given),
        out_specs=[VMEM] * chips,
        out_shape=[struct((rows, width))] * chips,
        compiler_params=PARAMS,
        name="core_join",
    )(where, *given)


def out_kernel(heads, where_ref, o_ref, m0, m1, m2, m3, own_ref, *refs):
    outs, full = refs[:-1], refs[-1]
    mixed, _, _ = join([m0, m1, m2, m3], heads)
    full[...] = mul(mixed, o_ref[...])
    width = own_ref.shape[1]
    for flip, out in enumerate((own_ref, *outs)):
        start = pl.multiple_of((where_ref[0] ^ flip) * width, width)
        out[...] = full[:, pl.ds(start, width)].astype(out.dtype)


def out_project(where, o_weight, messages, heads):
    rows = messages[0].shape[0] - 4 * heads
    width = o_weight.shape[1] // 4
    return pl.pallas_call(
        functools.partial(out_kernel, heads),
        in_specs=[SMEM] + [VMEM] * 5,
        out_specs=[VMEM] * 4,
        out_shape=[struct((rows, width), F32)] + [struct((rows, width))] * 3,
        scratch_shapes=[pltpu.VMEM((rows, o_weight.shape[1]), F32)],
        compiler_params=PARAMS,
        name="out_project",
    )(where, o_weight, *messages)


def move(value, hit_flip, head_flip):
    hits, heads = lax.axis_size("hit"), lax.axis_size("head")
    pairs = [
        (hit * heads + head, (hit ^ hit_flip) * heads + (head ^ head_flip))
        for hit in range(hits)
        for head in range(heads)
    ]
    return lax.ppermute(value, AXES, pairs)


def local_plane(slots, hits, hit_mask, q_weight, k_weight, v_weight, o_weight):
    width = q_weight.shape[1]
    heads = width // HEAD_DIM
    hit, head = lax.axis_index("hit"), lax.axis_index("head")
    where = jnp.stack([head, hit % 2, hit // 2, hit]).astype(jnp.int32)
    masks = hit_mask.reshape(4, 1, hits.shape[0])

    def mask_of(flip):
        return lax.dynamic_index_in_dim(masks, head ^ flip, 0, keepdims=False)

    ours = {}
    for flips in ((1, 2), (3, 0)):
        ours.update(zip(flips, project(flips, where, hits, k_weight, v_weight, width)))
    queries = query(slots, q_weight)
    theirs = {0: ours[0]}
    theirs.update((flip, move(ours[flip], 0, flip)) for flip in (1, 2))
    parts = []
    for flips in ((0,), (1, 2), (3,)):
        kept, sent = attend(
            where, queries, [theirs[flip] for flip in flips], [mask_of(flip) for flip in flips]
        )
        parts += [kept, move(sent, 1, 0)]
        if flips == (0,):
            ours[3], sent = lax.optimization_barrier((ours[3], sent))
            theirs[3] = move(ours[3], 0, 3)
    parts = core_join(where, parts, heads)
    messages = [parts[0]] + [move(parts[flip], 2 * flip, 0) for flip in (1, 2, 3)]
    shares = out_project(where, o_weight, messages, heads)
    total = shares[0]
    for flip in (1, 2, 3):
        total = total + move(shares[flip], 0, flip).astype(F32)
    return total.astype(BF16)


def attend_group(queries_head, keys_head, values_head, valid):
    scores = mul(queries_head, keys_head, NT) * HEAD_DIM ** (-0.5)
    scores = jnp.where(valid[None, :] > 0, scores, F32(-1e30))
    row_top = jnp.max(scores, axis=1)
    expo = jnp.exp(scores - row_top[:, None])
    totals = jnp.sum(expo, axis=1)
    return row_top, totals, mul(expo.astype(BF16), values_head)


def local_any(slots, hits, hit_mask, q_weight, k_weight, v_weight, o_weight):
    heads_here = q_weight.shape[1] // HEAD_DIM
    slot_count = slots.shape[0]
    queries = mul(slots, q_weight).astype(BF16)
    local_hits = hits.shape[0]
    head_devs = lax.axis_size("head")
    keys = mul(hits, k_weight).astype(BF16)
    values = mul(hits, v_weight).astype(BF16)
    keys = keys.reshape(local_hits, head_devs, heads_here, HEAD_DIM)
    values = values.reshape(local_hits, head_devs, heads_here, HEAD_DIM)
    both = jnp.concatenate([keys, values], axis=3)
    moved = lax.all_to_all(both, "head", split_axis=1, concat_axis=0, tiled=True)
    key_vals = moved.reshape(moved.shape[0], heads_here, 2 * HEAD_DIM)
    block = min(512, slot_count)
    row_tops, sums_list, partials = [], [], []
    for at in range(heads_here):
        queries_head = queries[:, at * HEAD_DIM : (at + 1) * HEAD_DIM]
        queries_head = queries_head.reshape(slot_count // block, block, HEAD_DIM)
        keys_head = key_vals[:, at, :HEAD_DIM]
        values_head = key_vals[:, at, HEAD_DIM:]
        head_top, head_sums, head_part = lax.map(
            lambda part: attend_group(part, keys_head, values_head, hit_mask), queries_head
        )
        row_tops.append(head_top.reshape(slot_count))
        sums_list.append(head_sums.reshape(slot_count))
        partials.append(head_part.reshape(slot_count, HEAD_DIM))
    row_top = jnp.stack(row_tops, axis=1)
    totals = jnp.stack(sums_list, axis=1)
    partial_value = jnp.concatenate(partials, axis=1)
    scale = jnp.exp(row_top - lax.pmax(row_top, "hit"))
    numer = lax.psum_scatter(
        partial_value * jnp.repeat(scale, HEAD_DIM, axis=1), "hit", scatter_dimension=0, tiled=True
    )
    denom = lax.psum_scatter(totals * scale, "hit", scatter_dimension=0, tiled=True)
    mixed = (numer / jnp.repeat(denom, HEAD_DIM, axis=1)).astype(BF16)
    head_terms = mul(mixed, o_weight)
    return lax.psum_scatter(head_terms, "head", scatter_dimension=1, tiled=True).astype(BF16)


def solution(mesh):
    placed = (P(), P(("hit", "head"), None), P("hit"), P(None, "head"), P(), P(), P("head", None))
    plane = mesh.shape["hit"] == 8 and mesh.shape["head"] == 4
    return jax.shard_map(
        local_plane if plane else local_any,
        mesh=mesh,
        in_specs=placed,
        out_specs=P("hit", "head"),
        check_vma=False,
    )
```

```python
import functools
import math

import jax
import jax.numpy as jnp
from jax import lax
from jax.experimental import pallas as pl
from jax.experimental.pallas import tpu as pltpu
from jax.sharding import PartitionSpec as P

HEAD_DIM = 64
F32 = jnp.float32
BF16 = jnp.bfloat16
NN = (((1,), (0,)), ((), ()))
NT = (((1,), (1,)), ((), ()))
SCALE = HEAD_DIM**-0.5 * math.log2(math.e)
AXES = ("hit", "head")
VMEM = pl.BlockSpec(memory_space=pltpu.VMEM)
HBM = pl.BlockSpec(memory_space=pltpu.HBM)
PARAMS = pltpu.CompilerParams(vmem_limit_bytes=40 << 20)


def mul(left, right, dims=NN):
    return lax.dot_general(left, right, dims, preferred_element_type=F32)


def struct(shape, dtype=BF16):
    return jax.ShapeDtypeStruct(shape, dtype)


def split(value, count):
    pieces = []
    for _ in range(count):
        piece = value.astype(BF16).astype(F32)
        pieces.append(piece)
        value = value - piece
    return pieces


def project_kernel(flips, hits_ref, k_ref, v_ref, *refs):
    outs = refs[: -len(PROJECT_SCRATCH)]
    hits_here, weights, in_sems = refs[-len(PROJECT_SCRATCH) :]
    width = weights.shape[2] // 2
    hits_copy = pltpu.make_async_copy(hits_ref, hits_here, in_sems.at[0, 0])
    hits_copy.start()
    copies = []
    for at, (flip, _) in enumerate(flips):
        columns = pl.ds(pl.multiple_of((lax.axis_index("head") ^ flip) * width, width), width)
        for side, source in enumerate((k_ref, v_ref)):
            target = weights.at[at, :, pl.ds(side * width, width)]
            copies.append(
                pltpu.make_async_copy(source.at[:, columns], target, in_sems.at[at + 1, side])
            )
            copies[-1].start()
    hits_copy.wait()
    for at, out in enumerate(outs):
        copies[2 * at].wait()
        copies[2 * at + 1].wait()
        out[...] = mul(hits_here[...], weights[at]).astype(BF16)


PROJECT_SCRATCH = ("hits", "weights", "in")


def project(flips, hits, k_weight, v_weight, width):
    rows, depth = hits.shape
    count = len(flips)
    shapes = [struct((rows // pieces, 2 * width)) for _, pieces in flips for _ in range(pieces)]
    outs = pl.pallas_call(
        functools.partial(project_kernel, flips),
        in_specs=[HBM, HBM, HBM],
        out_specs=[VMEM] * len(shapes),
        out_shape=shapes,
        scratch_shapes=[
            pltpu.VMEM((rows, depth), BF16),
            pltpu.VMEM((count, depth, 2 * width), BF16),
            pltpu.SemaphoreType.DMA((count + 1, 2)),
        ],
        compiler_params=pltpu.CompilerParams(vmem_limit_bytes=58 << 20),
        name="project" + "".join(str(flip) for flip, _ in flips),
    )(hits, k_weight, v_weight)
    taken = {}
    for flip, pieces in flips:
        taken[flip], outs = outs[:pieces], outs[pieces:]
    return taken


def query_kernel(slots_ref, q_ref, out_ref):
    rows = slots_ref.shape[0]
    queries = mul(slots_ref[...], q_ref[...]).astype(BF16).astype(F32)
    lane = lax.broadcasted_iota(jnp.int32, (rows, 128), 1)
    low = lane < HEAD_DIM
    for pair in range(queries.shape[1] // 128):
        pieces = split(queries[:, pair * 128 : (pair + 1) * 128] * SCALE, 3)
        rolled = [pltpu.roll(piece, HEAD_DIM, 1) for piece in pieces]
        one = jnp.where(lane == HEAD_DIM, 1.0, 0.0)
        out_ref[2 * pair, :, :128] = jnp.where(low, pieces[0], rolled[1]).astype(BF16)
        out_ref[2 * pair, :, 128:] = jnp.where(low, pieces[2], one).astype(BF16)
        out_ref[2 * pair + 1, :, :128] = jnp.where(low, rolled[0], pieces[1]).astype(BF16)
        out_ref[2 * pair + 1, :, 128:] = jnp.where(low, rolled[2], one).astype(BF16)


def query(slots, q_weight):
    rows, depth = slots.shape
    width = q_weight.shape[1]
    heads = width // HEAD_DIM
    block = 256
    return pl.pallas_call(
        query_kernel,
        grid=(rows // block,),
        in_specs=[
            pl.BlockSpec((block, depth), lambda i: (i, 0)),
            pl.BlockSpec((depth, width), lambda i: (0, 0)),
        ],
        out_specs=pl.BlockSpec((heads, block, 256), lambda i: (0, i, 0)),
        out_shape=struct((heads, rows, 256)),
        compiler_params=PARAMS,
        name="query",
    )(slots, q_weight)


def attend_kernel(count, *refs):
    q_ref = refs[0]
    kv_refs = refs[1 : 1 + count]
    mask_refs = refs[1 + count : 1 + 2 * count]
    keep_ref, send_ref, ke_ref, ve_ref, value_ref, stat_ref = refs[1 + 2 * count :]
    heads, slots = q_ref.shape[:2]
    pairs = heads // 2
    hits = kv_refs[0].shape[0]
    lane = lax.broadcasted_iota(jnp.int32, (hits, 128), 1)
    low = lane < HEAD_DIM
    for at in range(count):
        rows = pl.ds(at * hits, hits)
        off = jnp.where(mask_refs[at][...] > 0, 0.0, -1e30)
        column = jnp.broadcast_to(off, (128, hits)).T
        tail = jnp.where(lane == HEAD_DIM, column, 0.0)
        for pair in range(pairs):
            keys = kv_refs[at][:, pair * 128 : (pair + 1) * 128].astype(F32)
            rolled = pltpu.roll(keys, HEAD_DIM, 1)
            ke_ref[2 * pair, rows, :128] = jnp.where(low, keys, rolled).astype(BF16)
            ke_ref[2 * pair, rows, 128:] = jnp.where(low, keys, tail).astype(BF16)
            ke_ref[2 * pair + 1, rows, :128] = jnp.where(low, rolled, keys).astype(BF16)
            ke_ref[2 * pair + 1, rows, 128:] = jnp.where(low, rolled, tail).astype(BF16)
            start = (pairs + pair) * 128
            ve_ref[pair, rows, :128] = kv_refs[at][:, start : start + 128]
            ve_ref[pair, rows, 128:] = jnp.ones((hits, 128), BF16)
    block = 256
    half = block // 2
    slot_lane = lax.broadcasted_iota(jnp.int32, (block, 128), 1)
    slot_low = slot_lane < HEAD_DIM
    for step in range(slots // block):
        rows = pl.ds(step * block, block)
        stat = jnp.zeros((block, 128), F32)
        for pair in range(pairs):
            outs = []
            for head in (2 * pair, 2 * pair + 1):
                scores = mul(q_ref[head, rows, :], ke_ref[head], NT)
                top = jnp.max(scores, axis=1, keepdims=True)
                weights = jnp.exp2(scores - top).astype(BF16)
                both = mul(weights, ve_ref[pair])
                outs.append(both[:, :128])
                stat = jnp.where(slot_lane == head, top, stat)
                stat = jnp.where(slot_lane == 8 + head, both[:, 128:], stat)
            value = jnp.where(slot_low, outs[0], outs[1])
            value_ref[rows, pair * 128 : (pair + 1) * 128] = value.astype(BF16)
        stat_ref[rows, :] = stat
    core = lax.axis_index("hit") % 2
    for step in range(slots // block):
        for target, place in ((keep_ref, core), (send_ref, 1 - core)):
            part = pl.ds(pl.multiple_of(step * block + place * half, half), half)
            target[step, :half, :] = value_ref[part, :]
            flat = stat_ref[part, :].T
            target[step, half:, :] = pack(flat[:heads], flat[8 : 8 + heads])


def pack(top, total):
    heads, slots = top.shape
    gap = jnp.zeros((heads, slots), F32)
    left = jnp.concatenate(split(top, 3) + [gap], axis=0)
    right = jnp.concatenate(split(total, 2) + [gap, gap], axis=0)
    return jnp.concatenate([left, right], axis=1).astype(BF16)


def unpack(rows, heads):
    rows = rows.astype(F32)
    slots = rows.shape[1] // 2
    left, right = rows[:, :slots], rows[:, slots:]
    top = left[:heads] + left[heads : 2 * heads] + left[2 * heads : 3 * heads]
    total = right[:heads] + right[heads : 2 * heads]
    return top, total


def attend(queries, sources, masks):
    heads, slots, _ = queries.shape
    pairs = heads // 2
    count = len(sources)
    hits = sources[0].shape[0]
    block = 256
    message = struct((slots // block, block // 2 + 4 * heads, heads * HEAD_DIM))
    scores = heads * slots * count * hits
    return pl.pallas_call(
        functools.partial(attend_kernel, count),
        in_specs=[VMEM] * (1 + 2 * count),
        out_specs=(VMEM, VMEM),
        out_shape=(message, message),
        scratch_shapes=[
            pltpu.VMEM((heads, count * hits, 256), BF16),
            pltpu.VMEM((pairs, count * hits, 256), BF16),
            pltpu.VMEM((slots, heads * HEAD_DIM), BF16),
            pltpu.VMEM((slots, 128), F32),
        ],
        compiler_params=PARAMS,
        cost_estimate=pl.CostEstimate(
            flops=scores, bytes_accessed=1 << 20, transcendentals=0
        ),
        name=f"attend{count}",
    )(queries, *sources, *masks)


def spread(count, heads):
    shape = (256, count * heads * HEAD_DIM)
    row = lax.broadcasted_iota(jnp.int32, shape, 0) & 127
    column = lax.broadcasted_iota(jnp.int32, shape, 1) // HEAD_DIM
    return jnp.where(row == column, 1.0, 0.0).astype(BF16)


def join(messages, heads, matrix, final=False):
    slots = messages[0].shape[0] - 4 * heads
    width = heads * HEAD_DIM
    stats = [unpack(message[slots:, :], heads) for message in messages]
    top = functools.reduce(jnp.maximum, [one for one, _ in stats])
    rows = [jnp.exp2(one - top) for one, _ in stats]
    total = functools.reduce(jnp.add, [row * one for row, (_, one) in zip(rows, stats)])
    if final:
        rows = [row / total for row in rows]
    rows.append(jnp.zeros((128 - len(messages) * heads, slots), F32))
    factors = jnp.concatenate(split(jnp.concatenate(rows, axis=0).T, 2), axis=1)
    factors = mul(factors.astype(BF16), matrix)
    value = jnp.zeros((slots, width), F32)
    for at, message in enumerate(messages):
        value = value + message[:slots, :].astype(F32) * factors[:, at * width : (at + 1) * width]
    return value.astype(BF16), top, total


def early_kernel(heads, *refs):
    given, out = refs[:-1], refs[-1]
    slots = out.shape[1] - 4 * heads
    matrix = spread(len(given), heads)
    for place in range(out.shape[0]):
        value, top, total = join([one.at[place] for one in given], heads, matrix)
        out[place, :slots, :] = value
        out[place, slots:, :] = pack(top, total)


def early_join(given, heads):
    return pl.pallas_call(
        functools.partial(early_kernel, heads),
        in_specs=[VMEM] * len(given),
        out_specs=VMEM,
        out_shape=struct(given[0].shape),
        compiler_params=PARAMS,
        name="early_join",
    )(*given)


def core_kernel(heads, count, *refs):
    given, outs = refs[:count], refs[count:]
    slots = given[0].shape[1] - 4 * heads
    matrix = spread(count, heads)
    for flip, out in enumerate(outs):
        place = (lax.axis_index("hit") // 2) ^ flip
        value, top, total = join([one.at[place] for one in given], heads, matrix)
        out[:slots, :] = value
        out[slots:, :] = pack(top, total)


def core_join(given, heads):
    chips, rows, width = given[0].shape
    return pl.pallas_call(
        functools.partial(core_kernel, heads, len(given)),
        in_specs=[VMEM] * len(given),
        out_specs=[VMEM] * chips,
        out_shape=[struct((rows, width))] * chips,
        compiler_params=PARAMS,
        name="core_join",
    )(*given)


def out_kernel(heads, o_ref, m0, m1, m2, m3, own_ref, *refs):
    outs, full = refs[:-1], refs[-1]
    mixed, _, _ = join([m0, m1, m2, m3], heads, spread(4, heads), final=True)
    full[...] = mul(mixed, o_ref[...])
    width = own_ref.shape[1]
    for flip, out in enumerate((own_ref, *outs)):
        start = pl.multiple_of((lax.axis_index("head") ^ flip) * width, width)
        out[...] = full[:, pl.ds(start, width)].astype(out.dtype)


def out_project(o_weight, messages, heads):
    rows = messages[0].shape[0] - 4 * heads
    width = o_weight.shape[1] // 4
    return pl.pallas_call(
        functools.partial(out_kernel, heads),
        in_specs=[VMEM] * 5,
        out_specs=[VMEM] * 4,
        out_shape=[struct((rows, width), F32)] + [struct((rows, width))] * 3,
        scratch_shapes=[pltpu.VMEM((rows, o_weight.shape[1]), F32)],
        compiler_params=PARAMS,
        name="out_project",
    )(o_weight, *messages)


def move(value, hit_flip, head_flip):
    hits, heads = lax.axis_size("hit"), lax.axis_size("head")
    pairs = [
        (hit * heads + head, (hit ^ hit_flip) * heads + (head ^ head_flip))
        for hit in range(hits)
        for head in range(heads)
    ]
    return lax.ppermute(value, AXES, pairs)


def local_plane(slots, hits, hit_mask, q_weight, k_weight, v_weight, o_weight):
    width = q_weight.shape[1]
    heads = width // HEAD_DIM
    head = lax.axis_index("head")
    masks = hit_mask.reshape(4, 1, hits.shape[0])

    def mask_of(flip):
        return lax.dynamic_index_in_dim(masks, head ^ flip, 0, keepdims=False)

    ours = {}
    for flips in (((1, 1), (2, 1)), ((3, 1), (0, 1))):
        ours.update(project(flips, hits, k_weight, v_weight, width))
    queries = query(slots, q_weight)
    theirs = {flip: move(ours[flip][0], 0, flip) for flip in (1, 2)}
    mine = attend(queries, ours[0], [mask_of(0)])
    later = list(ours[3])
    later[0], mine, theirs = lax.optimization_barrier((later[0], mine, theirs))
    later = [move(piece, 0, 3) for piece in later]
    straight = attend(queries, [theirs[1], theirs[2]], [mask_of(1), mask_of(2)])
    parts = []
    for kept, sent in (mine, straight):
        parts += [kept, move(sent, 1, 0)]
    parts = [early_join(parts, heads)]
    queries, parts = lax.optimization_barrier((queries, parts))
    for at, piece in enumerate(later):
        size = piece.shape[0]
        mask = mask_of(3)[:, at * size : (at + 1) * size]
        kept, sent = attend(queries, [piece], [mask])
        parts += [kept, move(sent, 1, 0)]
    parts = core_join(parts, heads)
    messages = [parts[0]] + [move(parts[flip], 2 * flip, 0) for flip in (1, 2, 3)]
    shares = out_project(o_weight, messages, heads)
    total = shares[0]
    for flip in (1, 2, 3):
        total = total + move(shares[flip], 0, flip).astype(F32)
    return total.astype(BF16)


def attend_group(queries_head, keys_head, values_head, valid):
    scores = mul(queries_head, keys_head, NT) * HEAD_DIM ** (-0.5)
    scores = jnp.where(valid[None, :] > 0, scores, F32(-1e30))
    row_top = jnp.max(scores, axis=1)
    expo = jnp.exp(scores - row_top[:, None])
    totals = jnp.sum(expo, axis=1)
    return row_top, totals, mul(expo.astype(BF16), values_head)


def local_any(slots, hits, hit_mask, q_weight, k_weight, v_weight, o_weight):
    heads_here = q_weight.shape[1] // HEAD_DIM
    slot_count = slots.shape[0]
    queries = mul(slots, q_weight).astype(BF16)
    local_hits = hits.shape[0]
    head_devs = lax.axis_size("head")
    keys = mul(hits, k_weight).astype(BF16)
    values = mul(hits, v_weight).astype(BF16)
    keys = keys.reshape(local_hits, head_devs, heads_here, HEAD_DIM)
    values = values.reshape(local_hits, head_devs, heads_here, HEAD_DIM)
    both = jnp.concatenate([keys, values], axis=3)
    moved = lax.all_to_all(both, "head", split_axis=1, concat_axis=0, tiled=True)
    key_vals = moved.reshape(moved.shape[0], heads_here, 2 * HEAD_DIM)
    block = min(512, slot_count)
    row_tops, sums_list, partials = [], [], []
    for at in range(heads_here):
        queries_head = queries[:, at * HEAD_DIM : (at + 1) * HEAD_DIM]
        queries_head = queries_head.reshape(slot_count // block, block, HEAD_DIM)
        keys_head = key_vals[:, at, :HEAD_DIM]
        values_head = key_vals[:, at, HEAD_DIM:]
        head_top, head_sums, head_part = lax.map(
            lambda part: attend_group(part, keys_head, values_head, hit_mask), queries_head
        )
        row_tops.append(head_top.reshape(slot_count))
        sums_list.append(head_sums.reshape(slot_count))
        partials.append(head_part.reshape(slot_count, HEAD_DIM))
    row_top = jnp.stack(row_tops, axis=1)
    totals = jnp.stack(sums_list, axis=1)
    partial_value = jnp.concatenate(partials, axis=1)
    scale = jnp.exp(row_top - lax.pmax(row_top, "hit"))
    numer = lax.psum_scatter(
        partial_value * jnp.repeat(scale, HEAD_DIM, axis=1), "hit", scatter_dimension=0, tiled=True
    )
    denom = lax.psum_scatter(totals * scale, "hit", scatter_dimension=0, tiled=True)
    mixed = (numer / jnp.repeat(denom, HEAD_DIM, axis=1)).astype(BF16)
    head_terms = mul(mixed, o_weight)
    return lax.psum_scatter(head_terms, "head", scatter_dimension=1, tiled=True).astype(BF16)


def solution(mesh):
    placed = (P(), P(("hit", "head"), None), P("hit"), P(None, "head"), P(), P(), P("head", None))
    plane = mesh.shape["hit"] == 8 and mesh.shape["head"] == 4
    return jax.shard_map(
        local_plane if plane else local_any,
        mesh=mesh,
        in_specs=placed,
        out_specs=P("hit", "head"),
        check_vma=False,
    )
```

```python
import functools
import math

import jax
import jax.numpy as jnp
from jax import lax
from jax.experimental import pallas as pl
from jax.experimental.pallas import tpu as pltpu
from jax.sharding import PartitionSpec as P

HEAD_DIM = 64
F32 = jnp.float32
BF16 = jnp.bfloat16
NN = (((1,), (0,)), ((), ()))
NT = (((1,), (1,)), ((), ()))
SCALE = HEAD_DIM**-0.5 * math.log2(math.e)
AXES = ("hit", "head")
VMEM = pl.BlockSpec(memory_space=pltpu.VMEM)
HBM = pl.BlockSpec(memory_space=pltpu.HBM)
PARAMS = pltpu.CompilerParams(vmem_limit_bytes=40 << 20)


def mul(left, right, dims=NN):
    return lax.dot_general(left, right, dims, preferred_element_type=F32)


def struct(shape, dtype=BF16):
    return jax.ShapeDtypeStruct(shape, dtype)


def split(value, count):
    pieces = []
    for _ in range(count):
        piece = value.astype(BF16).astype(F32)
        pieces.append(piece)
        value = value - piece
    return pieces


def project_kernel(flips, hits_ref, k_ref, v_ref, *refs):
    outs = refs[: -len(PROJECT_SCRATCH)]
    hits_here, weights, in_sems = refs[-len(PROJECT_SCRATCH) :]
    width = weights.shape[2] // 2
    hits_copy = pltpu.make_async_copy(hits_ref, hits_here, in_sems.at[0, 0])
    hits_copy.start()
    copies = []
    for at, (flip, _) in enumerate(flips):
        columns = pl.ds(pl.multiple_of((lax.axis_index("head") ^ flip) * width, width), width)
        for side, source in enumerate((k_ref, v_ref)):
            target = weights.at[at, :, pl.ds(side * width, width)]
            copies.append(
                pltpu.make_async_copy(source.at[:, columns], target, in_sems.at[at + 1, side])
            )
            copies[-1].start()
    hits_copy.wait()
    place = 0
    for at, (_, pieces) in enumerate(flips):
        copies[2 * at].wait()
        copies[2 * at + 1].wait()
        both = mul(hits_here[...], weights[at]).astype(BF16)
        rows = both.shape[0] // pieces
        for piece in range(pieces):
            outs[place][...] = both[piece * rows : (piece + 1) * rows]
            place += 1


PROJECT_SCRATCH = ("hits", "weights", "in")


def project(flips, hits, k_weight, v_weight, width):
    rows, depth = hits.shape
    count = len(flips)
    shapes = [struct((rows // pieces, 2 * width)) for _, pieces in flips for _ in range(pieces)]
    outs = pl.pallas_call(
        functools.partial(project_kernel, flips),
        in_specs=[HBM, HBM, HBM],
        out_specs=[VMEM] * len(shapes),
        out_shape=shapes,
        scratch_shapes=[
            pltpu.VMEM((rows, depth), BF16),
            pltpu.VMEM((count, depth, 2 * width), BF16),
            pltpu.SemaphoreType.DMA((count + 1, 2)),
        ],
        compiler_params=pltpu.CompilerParams(vmem_limit_bytes=58 << 20),
        name="project" + "".join(str(flip) for flip, _ in flips),
    )(hits, k_weight, v_weight)
    taken = {}
    for flip, pieces in flips:
        taken[flip], outs = outs[:pieces], outs[pieces:]
    return taken


def query_kernel(slots_ref, q_ref, out_ref):
    rows = slots_ref.shape[0]
    queries = mul(slots_ref[...], q_ref[...]).astype(BF16).astype(F32)
    lane = lax.broadcasted_iota(jnp.int32, (rows, 128), 1)
    low = lane < HEAD_DIM
    for pair in range(queries.shape[1] // 128):
        pieces = split(queries[:, pair * 128 : (pair + 1) * 128] * SCALE, 3)
        rolled = [pltpu.roll(piece, HEAD_DIM, 1) for piece in pieces]
        one = jnp.where(lane == HEAD_DIM, 1.0, 0.0)
        out_ref[2 * pair, :, :128] = jnp.where(low, pieces[0], rolled[1]).astype(BF16)
        out_ref[2 * pair, :, 128:] = jnp.where(low, pieces[2], one).astype(BF16)
        out_ref[2 * pair + 1, :, :128] = jnp.where(low, rolled[0], pieces[1]).astype(BF16)
        out_ref[2 * pair + 1, :, 128:] = jnp.where(low, rolled[2], one).astype(BF16)


def query(slots, q_weight):
    rows, depth = slots.shape
    width = q_weight.shape[1]
    heads = width // HEAD_DIM
    block = 256
    return pl.pallas_call(
        query_kernel,
        grid=(rows // block,),
        in_specs=[
            pl.BlockSpec((block, depth), lambda i: (i, 0)),
            pl.BlockSpec((depth, width), lambda i: (0, 0)),
        ],
        out_specs=pl.BlockSpec((heads, block, 256), lambda i: (0, i, 0)),
        out_shape=struct((heads, rows, 256)),
        compiler_params=PARAMS,
        name="query",
    )(slots, q_weight)


def attend_kernel(count, sides, *refs):
    q_ref = refs[0]
    kv_refs = refs[1 : 1 + count]
    mask_refs = refs[1 + count : 1 + 2 * count]
    targets = refs[1 + 2 * count : -2]
    ke_ref, ve_ref = refs[-2:]
    heads = q_ref.shape[0]
    pairs = heads // 2
    hits = kv_refs[0].shape[0]
    lane = lax.broadcasted_iota(jnp.int32, (hits, 128), 1)
    low = lane < HEAD_DIM
    for at in range(count):
        rows = pl.ds(at * hits, hits)
        off = jnp.where(mask_refs[at][...] > 0, 0.0, -1e30)
        column = jnp.broadcast_to(off, (128, hits)).T
        tail = jnp.where(lane == HEAD_DIM, column, 0.0)
        for pair in range(pairs):
            keys = kv_refs[at][:, pair * 128 : (pair + 1) * 128].astype(F32)
            rolled = pltpu.roll(keys, HEAD_DIM, 1)
            ke_ref[2 * pair, rows, :128] = jnp.where(low, keys, rolled).astype(BF16)
            ke_ref[2 * pair, rows, 128:] = jnp.where(low, keys, tail).astype(BF16)
            ke_ref[2 * pair + 1, rows, :128] = jnp.where(low, rolled, keys).astype(BF16)
            ke_ref[2 * pair + 1, rows, 128:] = jnp.where(low, rolled, tail).astype(BF16)
            start = (pairs + pair) * 128
            ve_ref[pair, rows, :128] = kv_refs[at][:, start : start + 128]
            ve_ref[pair, rows, 128:] = jnp.ones((hits, 128), BF16)
    core = lax.axis_index("hit") % 2
    blocks = targets[0].shape[0]
    half = targets[0].shape[1] - 4 * heads
    slot_lane = lax.broadcasted_iota(jnp.int32, (2 * half, 128), 1)
    slot_low = slot_lane < HEAD_DIM
    for side, target in zip(sides, targets):
        place = core if side == "keep" else 1 - core
        for block in range(0, blocks, 2):
            rows = [
                pl.ds(pl.multiple_of((2 * (block + one) + place) * half, half), half)
                for one in range(2)
            ]
            stat = jnp.zeros((2 * half, 128), F32)
            for pair in range(pairs):
                outs = []
                for head in (2 * pair, 2 * pair + 1):
                    queries = jnp.concatenate([q_ref[head, one, :] for one in rows], axis=0)
                    scores = mul(queries, ke_ref[head], NT)
                    top = jnp.max(scores, axis=1, keepdims=True)
                    weights = jnp.exp2(scores - top).astype(BF16)
                    both = mul(weights, ve_ref[pair])
                    outs.append(both[:, :128])
                    stat = jnp.where(slot_lane == head, top, stat)
                    stat = jnp.where(slot_lane == 8 + head, both[:, 128:], stat)
                value = jnp.where(slot_low, outs[0], outs[1]).astype(BF16)
                for one in range(2):
                    target[block + one, :half, pair * 128 : (pair + 1) * 128] = value[
                        one * half : (one + 1) * half
                    ]
            for one in range(2):
                flat = stat[one * half : (one + 1) * half].T
                target[block + one, half:, :] = pack(flat[:heads], flat[8 : 8 + heads])


def pack(top, total):
    heads, slots = top.shape
    gap = jnp.zeros((heads, slots), F32)
    left = jnp.concatenate(split(top, 3) + [gap], axis=0)
    right = jnp.concatenate(split(total, 2) + [gap, gap], axis=0)
    return jnp.concatenate([left, right], axis=1).astype(BF16)


def unpack(rows, heads):
    rows = rows.astype(F32)
    slots = rows.shape[1] // 2
    left, right = rows[:, :slots], rows[:, slots:]
    top = left[:heads] + left[heads : 2 * heads] + left[2 * heads : 3 * heads]
    total = right[:heads] + right[heads : 2 * heads]
    return top, total


def attend(queries, sources, masks, sides=("keep", "send")):
    heads, slots, _ = queries.shape
    count = len(sources)
    hits = sources[0].shape[0]
    half = slots // (lax.axis_size("hit"))
    message = struct((lax.axis_size("hit") // 2, half + 4 * heads, heads * HEAD_DIM))
    scores = heads * slots * count * hits * len(sides) // 2
    return pl.pallas_call(
        functools.partial(attend_kernel, count, sides),
        in_specs=[VMEM] * (1 + 2 * count),
        out_specs=[VMEM] * len(sides),
        out_shape=[message] * len(sides),
        scratch_shapes=[
            pltpu.VMEM((heads, count * hits, 256), BF16),
            pltpu.VMEM((heads // 2, count * hits, 256), BF16),
        ],
        compiler_params=PARAMS,
        cost_estimate=pl.CostEstimate(flops=scores, bytes_accessed=1 << 20, transcendentals=0),
        name=f"attend{count}_" + "_".join(sides),
    )(queries, *sources, *masks)


def spread(count, heads):
    shape = (256, count * heads * HEAD_DIM)
    row = lax.broadcasted_iota(jnp.int32, shape, 0) & 127
    column = lax.broadcasted_iota(jnp.int32, shape, 1) // HEAD_DIM
    return jnp.where(row == column, 1.0, 0.0).astype(BF16)


def join(messages, heads, matrix, final=False):
    slots = messages[0].shape[0] - 4 * heads
    width = heads * HEAD_DIM
    stats = [unpack(message[slots:, :], heads) for message in messages]
    top = functools.reduce(jnp.maximum, [one for one, _ in stats])
    rows = [jnp.exp2(one - top) for one, _ in stats]
    total = functools.reduce(jnp.add, [row * one for row, (_, one) in zip(rows, stats)])
    if final:
        rows = [row / total for row in rows]
    rows.append(jnp.zeros((128 - len(messages) * heads, slots), F32))
    factors = jnp.concatenate(split(jnp.concatenate(rows, axis=0).T, 2), axis=1)
    factors = mul(factors.astype(BF16), matrix)
    value = jnp.zeros((slots, width), F32)
    for at, message in enumerate(messages):
        value = value + message[:slots, :].astype(F32) * factors[:, at * width : (at + 1) * width]
    return value.astype(BF16), top, total


def early_kernel(heads, *refs):
    given, out = refs[:-1], refs[-1]
    slots = out.shape[1] - 4 * heads
    matrix = spread(len(given), heads)
    for place in range(out.shape[0]):
        value, top, total = join([one.at[place] for one in given], heads, matrix)
        out[place, :slots, :] = value
        out[place, slots:, :] = pack(top, total)


def early_join(given, heads):
    return pl.pallas_call(
        functools.partial(early_kernel, heads),
        in_specs=[VMEM] * len(given),
        out_specs=VMEM,
        out_shape=struct(given[0].shape),
        compiler_params=PARAMS,
        name="early_join",
    )(*given)


def core_kernel(heads, count, *refs):
    given, outs = refs[:count], refs[count:]
    slots = given[0].shape[1] - 4 * heads
    matrix = spread(count, heads)
    for flip, out in enumerate(outs):
        place = (lax.axis_index("hit") // 2) ^ flip
        value, top, total = join([one.at[place] for one in given], heads, matrix)
        out[:slots, :] = value
        out[slots:, :] = pack(top, total)


def core_join(given, heads):
    chips, rows, width = given[0].shape
    return pl.pallas_call(
        functools.partial(core_kernel, heads, len(given)),
        in_specs=[VMEM] * len(given),
        out_specs=[VMEM] * chips,
        out_shape=[struct((rows, width))] * chips,
        compiler_params=PARAMS,
        name="core_join",
    )(*given)


def out_kernel(heads, o_ref, m0, m1, m2, m3, own_ref, *refs):
    outs, full = refs[:-1], refs[-1]
    mixed, _, _ = join([m0, m1, m2, m3], heads, spread(4, heads), final=True)
    full[...] = mul(mixed, o_ref[...])
    width = own_ref.shape[1]
    for flip, out in enumerate((own_ref, *outs)):
        start = pl.multiple_of((lax.axis_index("head") ^ flip) * width, width)
        out[...] = full[:, pl.ds(start, width)].astype(out.dtype)


def out_project(o_weight, messages, heads):
    rows = messages[0].shape[0] - 4 * heads
    width = o_weight.shape[1] // 4
    return pl.pallas_call(
        functools.partial(out_kernel, heads),
        in_specs=[VMEM] * 5,
        out_specs=[VMEM] * 4,
        out_shape=[struct((rows, width), F32)] + [struct((rows, width))] * 3,
        scratch_shapes=[pltpu.VMEM((rows, o_weight.shape[1]), F32)],
        compiler_params=PARAMS,
        name="out_project",
    )(o_weight, *messages)


def move(value, hit_flip, head_flip):
    hits, heads = lax.axis_size("hit"), lax.axis_size("head")
    pairs = [
        (hit * heads + head, (hit ^ hit_flip) * heads + (head ^ head_flip))
        for hit in range(hits)
        for head in range(heads)
    ]
    return lax.ppermute(value, AXES, pairs)


def local_plane(slots, hits, hit_mask, q_weight, k_weight, v_weight, o_weight):
    width = q_weight.shape[1]
    heads = width // HEAD_DIM
    head = lax.axis_index("head")
    masks = hit_mask.reshape(4, 1, hits.shape[0])

    def mask_of(flip):
        return lax.dynamic_index_in_dim(masks, head ^ flip, 0, keepdims=False)

    ours = {}
    for flips in (((1, 1), (2, 1)), ((3, 1), (0, 1))):
        ours.update(project(flips, hits, k_weight, v_weight, width))
    queries = query(slots, q_weight)
    theirs = {flip: move(ours[flip][0], 0, flip) for flip in (1, 2)}
    mine = attend(queries, ours[0], [mask_of(0)])
    later = list(ours[3])
    later[0], mine = lax.optimization_barrier((later[0], mine))
    later = [move(piece, 0, 3) for piece in later]
    theirs[2], theirs[1] = lax.optimization_barrier((theirs[2], theirs[1]))
    straight = attend(queries, [theirs[2], theirs[1]], [mask_of(2), mask_of(1)])
    parts = []
    for kept, sent in (mine, straight):
        parts += [kept, move(sent, 1, 0)]
    parts = [early_join(parts, heads)]
    queries, parts = lax.optimization_barrier((queries, parts))
    for at, piece in enumerate(later):
        size = piece.shape[0]
        mask = mask_of(3)[:, at * size : (at + 1) * size]
        (sent,) = attend(queries, [piece], [mask], ("send",))
        parts.append(move(sent, 1, 0))
        parts += attend(queries, [piece], [mask], ("keep",))
    parts = core_join(parts, heads)
    messages = [parts[0]] + [move(parts[flip], 2 * flip, 0) for flip in (1, 2, 3)]
    shares = out_project(o_weight, messages, heads)
    total = shares[0]
    for flip in (1, 2, 3):
        total = total + move(shares[flip], 0, flip).astype(F32)
    return total.astype(BF16)


def attend_group(queries_head, keys_head, values_head, valid):
    scores = mul(queries_head, keys_head, NT) * HEAD_DIM ** (-0.5)
    scores = jnp.where(valid[None, :] > 0, scores, F32(-1e30))
    row_top = jnp.max(scores, axis=1)
    expo = jnp.exp(scores - row_top[:, None])
    totals = jnp.sum(expo, axis=1)
    return row_top, totals, mul(expo.astype(BF16), values_head)


def local_any(slots, hits, hit_mask, q_weight, k_weight, v_weight, o_weight):
    heads_here = q_weight.shape[1] // HEAD_DIM
    slot_count = slots.shape[0]
    queries = mul(slots, q_weight).astype(BF16)
    local_hits = hits.shape[0]
    head_devs = lax.axis_size("head")
    keys = mul(hits, k_weight).astype(BF16)
    values = mul(hits, v_weight).astype(BF16)
    keys = keys.reshape(local_hits, head_devs, heads_here, HEAD_DIM)
    values = values.reshape(local_hits, head_devs, heads_here, HEAD_DIM)
    both = jnp.concatenate([keys, values], axis=3)
    moved = lax.all_to_all(both, "head", split_axis=1, concat_axis=0, tiled=True)
    key_vals = moved.reshape(moved.shape[0], heads_here, 2 * HEAD_DIM)
    block = min(512, slot_count)
    row_tops, sums_list, partials = [], [], []
    for at in range(heads_here):
        queries_head = queries[:, at * HEAD_DIM : (at + 1) * HEAD_DIM]
        queries_head = queries_head.reshape(slot_count // block, block, HEAD_DIM)
        keys_head = key_vals[:, at, :HEAD_DIM]
        values_head = key_vals[:, at, HEAD_DIM:]
        head_top, head_sums, head_part = lax.map(
            lambda part: attend_group(part, keys_head, values_head, hit_mask), queries_head
        )
        row_tops.append(head_top.reshape(slot_count))
        sums_list.append(head_sums.reshape(slot_count))
        partials.append(head_part.reshape(slot_count, HEAD_DIM))
    row_top = jnp.stack(row_tops, axis=1)
    totals = jnp.stack(sums_list, axis=1)
    partial_value = jnp.concatenate(partials, axis=1)
    scale = jnp.exp(row_top - lax.pmax(row_top, "hit"))
    numer = lax.psum_scatter(
        partial_value * jnp.repeat(scale, HEAD_DIM, axis=1), "hit", scatter_dimension=0, tiled=True
    )
    denom = lax.psum_scatter(totals * scale, "hit", scatter_dimension=0, tiled=True)
    mixed = (numer / jnp.repeat(denom, HEAD_DIM, axis=1)).astype(BF16)
    head_terms = mul(mixed, o_weight)
    return lax.psum_scatter(head_terms, "head", scatter_dimension=1, tiled=True).astype(BF16)


def solution(mesh):
    placed = (P(), P(("hit", "head"), None), P("hit"), P(None, "head"), P(), P(), P("head", None))
    plane = mesh.shape["hit"] == 8 and mesh.shape["head"] == 4
    return jax.shard_map(
        local_plane if plane else local_any,
        mesh=mesh,
        in_specs=placed,
        out_specs=P("hit", "head"),
        check_vma=False,
    )
```

```python
import functools
import math

import jax
import jax.numpy as jnp
from jax import lax
from jax.experimental import pallas as pl
from jax.experimental.pallas import tpu as pltpu
from jax.sharding import PartitionSpec as P

HEAD_DIM = 64
F32 = jnp.float32
BF16 = jnp.bfloat16
NN = (((1,), (0,)), ((), ()))
NT = (((1,), (1,)), ((), ()))
SCALE = HEAD_DIM**-0.5 * math.log2(math.e)
AXES = ("hit", "head")
VMEM = pl.BlockSpec(memory_space=pltpu.VMEM)
HBM = pl.BlockSpec(memory_space=pltpu.HBM)
PARAMS = pltpu.CompilerParams(vmem_limit_bytes=24 << 20)


def mul(left, right, dims=NN):
    return lax.dot_general(left, right, dims, preferred_element_type=F32)


def struct(shape, dtype=BF16):
    return jax.ShapeDtypeStruct(shape, dtype)


def split(value, count):
    pieces = []
    for _ in range(count):
        piece = value.astype(BF16).astype(F32)
        pieces.append(piece)
        value = value - piece
    return pieces


def project_kernel(flips, hits_ref, k_ref, v_ref, *refs):
    outs = refs[: len(flips)]
    hits_here, weights, both, in_sems, out_sems = refs[len(flips) :]
    width = weights.shape[2] // 2
    hits_copy = pltpu.make_async_copy(hits_ref, hits_here, in_sems.at[0, 0])
    hits_copy.start()
    copies = []
    for at, flip in enumerate(flips):
        start = (lax.axis_index("head") ^ flip) * width
        columns = pl.ds(pl.multiple_of(start, width), width)
        for side, source in enumerate((k_ref, v_ref)):
            target = weights.at[at, :, pl.ds(side * width, width)]
            copies.append(
                pltpu.make_async_copy(source.at[:, columns], target, in_sems.at[at + 1, side])
            )
            copies[-1].start()
    hits_copy.wait()
    leaving = []
    for at in range(len(flips)):
        copies[2 * at].wait()
        copies[2 * at + 1].wait()
        block = mul(hits_here[...], weights[at]).astype(BF16)
        both[at] = block
        leaving.append(pltpu.make_async_copy(both.at[at], outs[at], out_sems.at[at]))
        leaving[-1].start()
    for copy in leaving:
        copy.wait()


def project(flips, hits, k_weight, v_weight, width):
    rows, depth = hits.shape
    count = len(flips)
    block = (rows, 2 * width)
    outs = pl.pallas_call(
        functools.partial(project_kernel, flips),
        in_specs=[HBM, HBM, HBM],
        out_specs=[HBM] * count,
        out_shape=[struct(block)] * count,
        scratch_shapes=[
            pltpu.VMEM((rows, depth), BF16),
            pltpu.VMEM((count, depth, 2 * width), BF16),
            pltpu.VMEM((count, *block), BF16),
            pltpu.SemaphoreType.DMA((count + 1, 2)),
            pltpu.SemaphoreType.DMA((count,)),
        ],
        compiler_params=pltpu.CompilerParams(vmem_limit_bytes=58 << 20),
        name="project" + "".join(map(str, flips)),
    )(hits, k_weight, v_weight)
    return dict(zip(flips, outs))


def query_kernel(slots_ref, q_ref, out_ref):
    rows = slots_ref.shape[0]
    queries = mul(slots_ref[...], q_ref[...]).astype(BF16).astype(F32)
    lane = lax.broadcasted_iota(jnp.int32, (rows, 128), 1)
    low = lane < HEAD_DIM
    for pair in range(queries.shape[1] // 128):
        pieces = split(queries[:, pair * 128 : (pair + 1) * 128] * SCALE, 3)
        rolled = [pltpu.roll(piece, HEAD_DIM, 1) for piece in pieces]
        one = jnp.where(lane == HEAD_DIM, 1.0, 0.0)
        out_ref[2 * pair, :, :128] = jnp.where(low, pieces[0], rolled[1]).astype(BF16)
        out_ref[2 * pair, :, 128:] = jnp.where(low, pieces[2], one).astype(BF16)
        out_ref[2 * pair + 1, :, :128] = jnp.where(low, rolled[0], pieces[1]).astype(BF16)
        out_ref[2 * pair + 1, :, 128:] = jnp.where(low, rolled[2], one).astype(BF16)


def query(slots, q_weight):
    rows, depth = slots.shape
    width = q_weight.shape[1]
    heads = width // HEAD_DIM
    block = 256
    return pl.pallas_call(
        query_kernel,
        grid=(rows // block,),
        in_specs=[
            pl.BlockSpec((block, depth), lambda i: (i, 0)),
            pl.BlockSpec((depth, width), lambda i: (0, 0)),
        ],
        out_specs=pl.BlockSpec((heads, block, 256), lambda i: (0, i, 0)),
        out_shape=struct((heads, rows, 256)),
        compiler_params=PARAMS,
        name="query",
    )(slots, q_weight)


def extend(kv_refs, mask_refs, ke_ref, ve_ref):
    pairs = ve_ref.shape[0]
    hits = kv_refs[0].shape[0]
    lane = lax.broadcasted_iota(jnp.int32, (hits, 128), 1)
    low = lane < HEAD_DIM
    for at in range(len(kv_refs)):
        rows = pl.ds(at * hits, hits)
        off = jnp.where(mask_refs[at][...] > 0, 0.0, -1e30)
        column = jnp.broadcast_to(off, (128, hits)).T
        tail = jnp.where(lane == HEAD_DIM, column, 0.0)
        for pair in range(pairs):
            keys = kv_refs[at][:, pair * 128 : (pair + 1) * 128].astype(F32)
            rolled = pltpu.roll(keys, HEAD_DIM, 1)
            ke_ref[2 * pair, rows, :128] = jnp.where(low, keys, rolled).astype(BF16)
            ke_ref[2 * pair, rows, 128:] = jnp.where(low, keys, tail).astype(BF16)
            ke_ref[2 * pair + 1, rows, :128] = jnp.where(low, rolled, keys).astype(BF16)
            ke_ref[2 * pair + 1, rows, 128:] = jnp.where(low, rolled, tail).astype(BF16)
            start = (pairs + pair) * 128
            ve_ref[pair, rows, :128] = kv_refs[at][:, start : start + 128]
            ve_ref[pair, rows, 128:] = jnp.ones((hits, 128), BF16)


def attend_kernel(count, sides, given, *refs):
    q_ref = refs[0]
    heads = q_ref.shape[0]
    pairs = heads // 2
    if given:
        ke_ref, ve_ref, *targets = refs[1:]
    else:
        kv_refs = refs[1 : 1 + count]
        mask_refs = refs[1 + count : 1 + 2 * count]
        *targets, ke_ref, ve_ref = refs[1 + 2 * count :]
        extend(kv_refs, mask_refs, ke_ref, ve_ref)
    core = lax.axis_index("hit") % 2
    blocks = targets[0].shape[0]
    half = targets[0].shape[1] - 4 * heads
    slot_lane = lax.broadcasted_iota(jnp.int32, (2 * half, 128), 1)
    slot_low = slot_lane < HEAD_DIM
    for side, target in zip(sides, targets):
        place = core if side == "keep" else 1 - core
        for block in range(0, blocks, 2):
            rows = [
                pl.ds(pl.multiple_of((2 * (block + one) + place) * half, half), half)
                for one in range(2)
            ]
            stat = jnp.zeros((2 * half, 128), F32)
            for pair in range(pairs):
                outs = []
                for head in (2 * pair, 2 * pair + 1):
                    queries = jnp.concatenate([q_ref[head, one, :] for one in rows], axis=0)
                    scores = mul(queries, ke_ref[head], NT)
                    top = jnp.max(scores, axis=1, keepdims=True)
                    weights = jnp.exp2(scores - top).astype(BF16)
                    both = mul(weights, ve_ref[pair])
                    outs.append(both[:, :128])
                    stat = jnp.where(slot_lane == head, top, stat)
                    stat = jnp.where(slot_lane == 8 + head, both[:, 128:], stat)
                value = jnp.where(slot_low, outs[0], outs[1]).astype(BF16)
                for one in range(2):
                    target[block + one, :half, pair * 128 : (pair + 1) * 128] = value[
                        one * half : (one + 1) * half
                    ]
            for one in range(2):
                flat = stat[one * half : (one + 1) * half].T
                target[block + one, half:, :] = pack(flat[:heads], flat[8 : 8 + heads])


def pack(top, total):
    heads, slots = top.shape
    gap = jnp.zeros((heads, slots), F32)
    left = jnp.concatenate(split(top, 3) + [gap], axis=0)
    right = jnp.concatenate(split(total, 2) + [gap, gap], axis=0)
    return jnp.concatenate([left, right], axis=1).astype(BF16)


def unpack(rows, heads):
    rows = rows.astype(F32)
    slots = rows.shape[1] // 2
    left, right = rows[:, :slots], rows[:, slots:]
    top = left[:heads] + left[heads : 2 * heads] + left[2 * heads : 3 * heads]
    total = right[:heads] + right[heads : 2 * heads]
    return top, total


def attend(queries, sources, masks, sides=("keep", "send"), given=(), give=False):
    heads, slots, _ = queries.shape
    count = len(sources)
    half = slots // lax.axis_size("hit")
    message = struct((lax.axis_size("hit") // 2, half + 4 * heads, heads * HEAD_DIM))
    outs = [message] * len(sides)
    scratch = []
    if not given:
        hits = sum(source.shape[0] for source in sources)
        scratch = [pltpu.VMEM((heads, hits, 256), BF16), pltpu.VMEM((heads // 2, hits, 256), BF16)]
    if give:
        outs, scratch = outs + scratch, []
    operands = given if given else (*sources, *masks)
    return pl.pallas_call(
        functools.partial(attend_kernel, count, sides, bool(given)),
        in_specs=[VMEM] * (1 + len(operands)),
        out_specs=[VMEM] * len(outs),
        out_shape=outs,
        scratch_shapes=scratch,
        compiler_params=PARAMS,
        cost_estimate=pl.CostEstimate(
            flops=heads * slots * 1024, bytes_accessed=1 << 20, transcendentals=0
        ),
        name=f"attend{count}_" + "_".join(sides),
    )(queries, *operands)


def spread(count, heads):
    shape = (256, count * heads * HEAD_DIM)
    row = lax.broadcasted_iota(jnp.int32, shape, 0) & 127
    column = lax.broadcasted_iota(jnp.int32, shape, 1) // HEAD_DIM
    return jnp.where(row == column, 1.0, 0.0).astype(BF16)


def join(messages, heads, matrix, final=False):
    slots = messages[0].shape[0] - 4 * heads
    width = heads * HEAD_DIM
    stats = [unpack(message[slots:, :], heads) for message in messages]
    top = functools.reduce(jnp.maximum, [one for one, _ in stats])
    rows = [jnp.exp2(one - top) for one, _ in stats]
    total = functools.reduce(jnp.add, [row * one for row, (_, one) in zip(rows, stats)])
    if final:
        rows = [row / total for row in rows]
    rows.append(jnp.zeros((128 - len(messages) * heads, slots), F32))
    factors = jnp.concatenate(split(jnp.concatenate(rows, axis=0).T, 2), axis=1)
    factors = mul(factors.astype(BF16), matrix)
    value = jnp.zeros((slots, width), F32)
    for at, message in enumerate(messages):
        value = value + message[:slots, :].astype(F32) * factors[:, at * width : (at + 1) * width]
    return value.astype(BF16), top, total


def early_kernel(heads, *refs):
    given, out = refs[:-1], refs[-1]
    slots = out.shape[1] - 4 * heads
    matrix = spread(len(given), heads)
    for place in range(out.shape[0]):
        value, top, total = join([one.at[place] for one in given], heads, matrix)
        out[place, :slots, :] = value
        out[place, slots:, :] = pack(top, total)


def early_join(given, heads):
    return pl.pallas_call(
        functools.partial(early_kernel, heads),
        in_specs=[VMEM] * len(given),
        out_specs=VMEM,
        out_shape=struct(given[0].shape),
        compiler_params=PARAMS,
        name="early_join",
    )(*given)


def core_kernel(heads, count, *refs):
    given, outs = refs[:count], refs[count:]
    slots = given[0].shape[1] - 4 * heads
    matrix = spread(count, heads)
    for flip, out in enumerate(outs):
        place = (lax.axis_index("hit") // 2) ^ flip
        value, top, total = join([one.at[place] for one in given], heads, matrix)
        out[:slots, :] = value
        out[slots:, :] = pack(top, total)


def core_join(given, heads):
    chips, rows, width = given[0].shape
    return pl.pallas_call(
        functools.partial(core_kernel, heads, len(given)),
        in_specs=[VMEM] * len(given),
        out_specs=[VMEM] * chips,
        out_shape=[struct((rows, width))] * chips,
        compiler_params=PARAMS,
        name="core_join",
    )(*given)


def out_kernel(heads, o_ref, m0, m1, m2, m3, own_ref, *refs):
    outs, full = refs[:-1], refs[-1]
    mixed, _, _ = join([m0, m1, m2, m3], heads, spread(4, heads), final=True)
    full[...] = mul(mixed, o_ref[...])
    width = own_ref.shape[1]
    for flip, out in enumerate((own_ref, *outs)):
        start = pl.multiple_of((lax.axis_index("head") ^ flip) * width, width)
        out[...] = full[:, pl.ds(start, width)].astype(out.dtype)


def out_project(o_weight, messages, heads):
    rows = messages[0].shape[0] - 4 * heads
    width = o_weight.shape[1] // 4
    return pl.pallas_call(
        functools.partial(out_kernel, heads),
        in_specs=[VMEM] * 5,
        out_specs=[VMEM] * 4,
        out_shape=[struct((rows, width), F32)] + [struct((rows, width))] * 3,
        scratch_shapes=[pltpu.VMEM((rows, o_weight.shape[1]), F32)],
        compiler_params=PARAMS,
        name="out_project",
    )(o_weight, *messages)


def move(value, hit_flip, head_flip):
    hits, heads = lax.axis_size("hit"), lax.axis_size("head")
    pairs = [
        (hit * heads + head, (hit ^ hit_flip) * heads + (head ^ head_flip))
        for hit in range(hits)
        for head in range(heads)
    ]
    return lax.ppermute(value, AXES, pairs)


def local_plane(slots, hits, hit_mask, q_weight, k_weight, v_weight, o_weight):
    width = q_weight.shape[1]
    heads = width // HEAD_DIM
    head = lax.axis_index("head")
    masks = hit_mask.reshape(4, 1, hits.shape[0])

    def mask_of(flip):
        return lax.dynamic_index_in_dim(masks, head ^ flip, 0, keepdims=False)

    ours = {}
    for flips in ((1, 2), (3, 0)):
        ours.update(project(flips, hits, k_weight, v_weight, width))
    queries = query(slots, q_weight)
    theirs = {flip: move(ours[flip], 0, flip) for flip in (1, 2)}
    mine = attend(queries, [ours[0]], [mask_of(0)])
    later = [ours[3]]
    later[0], mine = lax.optimization_barrier((later[0], mine))
    later = [move(piece, 0, 3) for piece in later]
    theirs[2], theirs[1] = lax.optimization_barrier((theirs[2], theirs[1]))
    straight = attend(queries, [theirs[2], theirs[1]], [mask_of(2), mask_of(1)])
    parts = []
    for kept, sent in (mine, straight):
        parts += [kept, move(sent, 1, 0)]
    parts = [early_join(parts, heads)]
    queries, parts = lax.optimization_barrier((queries, parts))
    for at, piece in enumerate(later):
        size = piece.shape[0]
        mask = mask_of(3)[:, at * size : (at + 1) * size]
        sent, *rows = attend(queries, [piece], [mask], ("send",), give=True)
        parts.append(move(sent, 1, 0))
        parts += attend(queries, (), (), ("keep",), given=rows)
    parts = core_join(parts, heads)
    messages = [parts[0]] + [move(parts[flip], 2 * flip, 0) for flip in (1, 2, 3)]
    shares = out_project(o_weight, messages, heads)
    total = shares[0]
    for flip in (1, 2, 3):
        total = total + move(shares[flip], 0, flip).astype(F32)
    return total.astype(BF16)


def attend_group(queries_head, keys_head, values_head, valid):
    scores = mul(queries_head, keys_head, NT) * HEAD_DIM ** (-0.5)
    scores = jnp.where(valid[None, :] > 0, scores, F32(-1e30))
    row_top = jnp.max(scores, axis=1)
    expo = jnp.exp(scores - row_top[:, None])
    totals = jnp.sum(expo, axis=1)
    return row_top, totals, mul(expo.astype(BF16), values_head)


def local_any(slots, hits, hit_mask, q_weight, k_weight, v_weight, o_weight):
    heads_here = q_weight.shape[1] // HEAD_DIM
    slot_count = slots.shape[0]
    queries = mul(slots, q_weight).astype(BF16)
    local_hits = hits.shape[0]
    head_devs = lax.axis_size("head")
    keys = mul(hits, k_weight).astype(BF16)
    values = mul(hits, v_weight).astype(BF16)
    keys = keys.reshape(local_hits, head_devs, heads_here, HEAD_DIM)
    values = values.reshape(local_hits, head_devs, heads_here, HEAD_DIM)
    both = jnp.concatenate([keys, values], axis=3)
    moved = lax.all_to_all(both, "head", split_axis=1, concat_axis=0, tiled=True)
    key_vals = moved.reshape(moved.shape[0], heads_here, 2 * HEAD_DIM)
    block = min(512, slot_count)
    row_tops, sums_list, partials = [], [], []
    for at in range(heads_here):
        queries_head = queries[:, at * HEAD_DIM : (at + 1) * HEAD_DIM]
        queries_head = queries_head.reshape(slot_count // block, block, HEAD_DIM)
        keys_head = key_vals[:, at, :HEAD_DIM]
        values_head = key_vals[:, at, HEAD_DIM:]
        head_top, head_sums, head_part = lax.map(
            lambda part: attend_group(part, keys_head, values_head, hit_mask), queries_head
        )
        row_tops.append(head_top.reshape(slot_count))
        sums_list.append(head_sums.reshape(slot_count))
        partials.append(head_part.reshape(slot_count, HEAD_DIM))
    row_top = jnp.stack(row_tops, axis=1)
    totals = jnp.stack(sums_list, axis=1)
    partial_value = jnp.concatenate(partials, axis=1)
    scale = jnp.exp(row_top - lax.pmax(row_top, "hit"))
    numer = lax.psum_scatter(
        partial_value * jnp.repeat(scale, HEAD_DIM, axis=1), "hit", scatter_dimension=0, tiled=True
    )
    denom = lax.psum_scatter(totals * scale, "hit", scatter_dimension=0, tiled=True)
    mixed = (numer / jnp.repeat(denom, HEAD_DIM, axis=1)).astype(BF16)
    head_terms = mul(mixed, o_weight)
    return lax.psum_scatter(head_terms, "head", scatter_dimension=1, tiled=True).astype(BF16)


def solution(mesh):
    placed = (P(), P(("hit", "head"), None), P("hit"), P(None, "head"), P(), P(), P("head", None))
    plane = mesh.shape["hit"] == 8 and mesh.shape["head"] == 4
    return jax.shard_map(
        local_plane if plane else local_any,
        mesh=mesh,
        in_specs=placed,
        out_specs=P("hit", "head"),
        check_vma=False,
    )
```
